256 devices in a mesh: store: 128 (over y_hi, z, x, core), pair: 2 (over y_lo).
Axes of the slice: x: 4, y: 4 (y_hi: 2, y_lo: 2; y = y_hi * 2 + y_lo), z: 8, core: 2. Of those that a mesh axis runs over, the one named last changes fastest.
Arguments:
- queries: bfloat16 [128, 2, 2, 128, 8192], P('store', 'pair'), may hold values from -6 to 6
- suffix_keys: bfloat16 [128, 2, 2, 128, 1024], P('store', 'pair'), may hold values from -6 to 6
- suffix_values: bfloat16 [128, 2, 2, 128, 1024], P('store', 'pair'), may hold values from -6 to 6
- page_keys: bfloat16 [8192, 8, 1024], P('store'), may hold values from -6 to 6
- page_values: bfloat16 [8192, 8, 1024], P('store'), may hold values from -6 to 6
- leaf_parent: int32 [64], replicated, may hold values from 0 to 15
- node_pages: int32 [81], replicated, may hold values from 1 to 64, as said below
- page_slot: int32 [81, 64], replicated, may hold values from 0 to 8191, as said below
- request_leaf: int32 [128], replicated, may hold values from 0 to 63
- prefix_len: int32 [128], replicated, may hold values from 1 to 1024, as said below
Outputs:
- attended: bfloat16 [128, 2, 2, 128, 8192], P('store', 'pair')
The draws below stay inside these ranges and needn't reach their ends.
Inputs may be any that keep to these rules, and one draw needn't show every extreme that they name: `node_pages`: entry 0 is the root with at most 32 pages, entries 1 to 16 are the middle nodes with at most 32 pages, the others are the leaves with at most 64. `page_slot`: entries [n, i] with i at or above node n's page count are 0; all other entries are distinct; place g lies on store index g // 64; the pages of one request's path lie at most 1 to a store index, and some request's path reaches 1. `prefix_len`: at least half of the request's path tokens and at most all of them.
All inputs are finite; a program needn't handle non-finite values.
Results may differ from the reference program's by a relative error of at most 0.008.
Values may be sent and summed in bfloat16 or wider, within the bound.
A program may use at most 128 MiB of HBM per device.

```python
import jax
import jax.numpy as jnp
from jax import lax

QH = 64
KVH = 8
HD = 128
SUF = 512
PAGE = 8
PREFIX_PG = 128
REQUESTS = 128
BLK = 128
MIDS = 16
LEAVES = 64
ROOT_MOST = 32
MID_MOST = 32
LEAF_MOST = 64
PAGES_DEV = 64
PAGES = 8192
N_STORE = 128
N_PAIR = 2


def tree_draw(key):
    keys = jax.random.split(jax.random.fold_in(key, 5), 11)
    leaf_parent = jax.random.randint(keys[0], (LEAVES,), 0, MIDS)
    first_pick = jax.random.randint(keys[1], (REQUESTS,), 0, LEAVES)
    second_pick = jax.random.randint(keys[2], (REQUESTS,), 0, LEAVES)
    shuffle = jax.random.permutation(keys[3], LEAVES).astype(jnp.int32)
    request_leaf = jnp.take(shuffle, jnp.minimum(first_pick, second_pick)).astype(jnp.int32)
    root_count = jnp.full((1,), ROOT_MOST, jnp.int32)
    mid_count = jax.random.randint(keys[5], (MIDS,), 1, MID_MOST + 1)
    leaf_count = jax.random.randint(keys[6], (LEAVES,), 1, LEAF_MOST + 1)
    leaf_ids = jnp.arange(LEAVES, dtype=jnp.int32)
    chosen = request_leaf[0]
    leaf_count = jnp.where(leaf_ids == chosen, LEAF_MOST, jnp.where(leaf_ids == (chosen + 1) % LEAVES, 1, leaf_count))
    mid_ids = jnp.arange(MIDS, dtype=jnp.int32)
    mid_count = jnp.where(mid_ids == leaf_parent[chosen], MID_MOST, mid_count)
    node_pages = jnp.concatenate([root_count, mid_count, leaf_count]).astype(jnp.int32)

    def lay_out(level_counts, band_start, band_width, perm_key):
        starts = jnp.cumsum(level_counts) - level_counts
        flat_index = starts[:, None] + jnp.arange(LEAF_MOST, dtype=jnp.int32)[None, :]
        band_order = jax.random.permutation(perm_key, band_width).astype(jnp.int32)
        holder = band_start + jnp.take(band_order, flat_index % band_width)
        local_row = flat_index // band_width
        used = jnp.arange(LEAF_MOST, dtype=jnp.int32)[None, :] < level_counts[:, None]
        return jnp.where(used, holder * PAGES_DEV + local_row, 0).astype(jnp.int32)
    quarter = N_STORE // 4
    page_slot = jnp.concatenate([lay_out(root_count, 0, quarter, keys[7]), lay_out(mid_count, quarter, quarter, keys[8]), lay_out(leaf_count, 2 * quarter, 2 * quarter, keys[9])], axis=0)
    path_tokens = PAGE * (root_count[0] + jnp.take(mid_count, jnp.take(leaf_parent, request_leaf)) + jnp.take(leaf_count, request_leaf))
    cut_tokens = jax.random.randint(keys[10], (REQUESTS,), 0, path_tokens // 2 + 1)
    cut_tokens = jnp.where(jnp.arange(REQUESTS, dtype=jnp.int32) == 0, 0, cut_tokens)
    prefix_len = (path_tokens - cut_tokens).astype(jnp.int32)
    return (leaf_parent.astype(jnp.int32), node_pages, page_slot, request_leaf, prefix_len)


def draw_leaf_parent(key, part):
    return tree_draw(key)[0]


def draw_node_pages(key, part):
    return tree_draw(key)[1]


def draw_page_slot(key, part):
    return tree_draw(key)[2]


def draw_request_leaf(key, part):
    return tree_draw(key)[3]


def draw_prefix_len(key, part):
    return tree_draw(key)[4]


def draw_queries(key, part):
    shape = (REQUESTS, N_PAIR, 2, BLK, QH * HD)
    key = jax.random.fold_in(key, 11)
    return jax.random.truncated_normal(key, -6.0, 6.0, shape).astype(jnp.bfloat16)


def draw_suffix_keys(key, part):
    shape = (REQUESTS, N_PAIR, 2, BLK, KVH * HD)
    key = jax.random.fold_in(key, 12)
    return jax.random.truncated_normal(key, -6.0, 6.0, shape).astype(jnp.bfloat16)


def block_scale(own_key, extent, cuts, low, top_value):
    factor_of, own = 1.0, jax.random.fold_in(own_key, 6)
    for axis_at, shards_of in cuts:
        draws = jnp.exp(jax.random.uniform(jax.random.fold_in(own, axis_at), (shards_of,), jnp.float32, low / len(cuts), top_value / len(cuts)))
        factor_of = factor_of * jnp.repeat(draws, extent[axis_at] // shards_of).reshape([-1 if axis == axis_at else 1 for axis in range(len(extent))])
    return factor_of


def centred(key, dims, spread, most, pieces=(), kind=jnp.bfloat16):
    loudness = block_scale(key, dims, pieces, -0.22, 0.18) if pieces else 1.0
    values = jax.random.normal(key, dims, jnp.float32) * spread * loudness
    return jnp.minimum(jnp.maximum(values, -most), most).astype(kind)


def setup_inputs(seed: int = 0) -> dict:
    key_list = jax.random.split(jax.random.key(seed), 11)
    queries = draw_queries(jax.random.fold_in(key_list[10], 71), 0)
    suffix_keys = draw_suffix_keys(jax.random.fold_in(key_list[10], 71), 0)
    suffix_values = centred(key_list[2], (REQUESTS, N_PAIR, 2, BLK, KVH * HD), 1.0, 6.0, ((0, 128), (1, 2)))
    page_keys = centred(key_list[3], (PAGES, PAGE, KVH * HD), 1.0, 6.0, ((0, 128),))
    page_values = centred(key_list[4], (PAGES, PAGE, KVH * HD), 1.0, 6.0, ((0, 128),))
    leaf_parent = draw_leaf_parent(jax.random.fold_in(key_list[10], 71), 0)
    node_pages = draw_node_pages(jax.random.fold_in(key_list[10], 71), 0)
    page_slot = draw_page_slot(jax.random.fold_in(key_list[10], 71), 0)
    request_leaf = draw_request_leaf(jax.random.fold_in(key_list[10], 71), 0)
    prefix_len = draw_prefix_len(jax.random.fold_in(key_list[10], 71), 0)
    return dict(queries=queries, suffix_keys=suffix_keys, suffix_values=suffix_values, page_keys=page_keys, page_values=page_values, leaf_parent=leaf_parent, node_pages=node_pages, page_slot=page_slot, request_leaf=request_leaf, prefix_len=prefix_len)


def path_table(leaf_parent, node_pages, page_slot, request_leaf, prefix_len):
    mids = node_pages.shape[0] - 1 - leaf_parent.shape[0]
    row_width = page_slot.shape[1]
    leaf_node = 1 + mids + request_leaf
    mid_node = 1 + jnp.take(leaf_parent, request_leaf)
    root_count = node_pages[0]
    mid_count = jnp.take(node_pages, mid_node)[:, None]
    leaf_count = jnp.take(node_pages, leaf_node)[:, None]
    page_order = jnp.arange(PREFIX_PG, dtype=jnp.int32)[None, :]
    in_root = page_order < root_count
    in_mid = page_order < root_count + mid_count
    node_ids = jnp.where(in_root, 0, jnp.where(in_mid, mid_node[:, None], leaf_node[:, None]))
    within = jnp.where(in_root, page_order, jnp.where(in_mid, page_order - root_count, page_order - root_count - mid_count))
    in_use = (page_order < root_count + mid_count + leaf_count) & (page_order * PAGE < prefix_len[:, None])
    within = jnp.where(in_use, within, 0)
    page_ids = jnp.take(page_slot.reshape(-1), (node_ids * row_width + within).astype(jnp.int32))
    return jnp.where(in_use, page_ids, 0).astype(jnp.int32), in_use


def mirror_positions(pairs, block_rows):
    pair_ids = jnp.arange(pairs, dtype=jnp.int32)[:, None, None]
    half_ids = jnp.arange(2, dtype=jnp.int32)[None, :, None]
    block_ids = jnp.where(half_ids == 0, pair_ids, 2 * pairs - 1 - pair_ids)
    return (block_ids * block_rows + jnp.arange(block_rows, dtype=jnp.int32)[None, None, :]).reshape(-1)


def reference(queries, suffix_keys, suffix_values, page_keys, page_values, leaf_parent, node_pages, page_slot, request_leaf, prefix_len):
    page_ids, in_use = path_table(leaf_parent, node_pages, page_slot, request_leaf, prefix_len)
    positions = mirror_positions(N_PAIR, BLK)
    group_size = QH // KVH
    score_scale = HD ** -0.5
    prefix_tokens = PREFIX_PG * PAGE
    token_pos = jnp.arange(prefix_tokens, dtype=jnp.int32)
    causal = positions[None, :] <= positions[:, None]

    def per_request(request):
        query_heads = queries[request].reshape(SUF, KVH, group_size, HD).astype(jnp.float32)
        own_keys = suffix_keys[request].reshape(SUF, KVH, HD)
        own_values = suffix_values[request].reshape(SUF, KVH, HD)
        path_keys = jnp.take(page_keys, page_ids[request], axis=0).reshape(prefix_tokens, KVH, HD)
        path_values = jnp.take(page_values, page_ids[request], axis=0).reshape(prefix_tokens, KVH, HD)
        visible = jnp.repeat(in_use[request], PAGE) & (token_pos < prefix_len[request])
        all_keys = jnp.concatenate([path_keys, own_keys], axis=0).astype(jnp.float32)
        all_values = jnp.concatenate([path_values, own_values], axis=0).astype(jnp.float32)
        allowed = jnp.concatenate([jnp.broadcast_to(visible[None, :], (SUF, prefix_tokens)), causal], axis=1)
        scores = jnp.einsum("qhgd,khd->hgqk", query_heads, all_keys) * score_scale
        scores = jnp.where(allowed[None, None], scores, -1e30)
        row_max = jnp.max(scores, axis=-1, keepdims=True)
        weights = jnp.exp(scores - row_max)
        row_total = jnp.sum(weights, axis=-1)
        rounded = lax.optimization_barrier(weights.astype(jnp.bfloat16)).astype(jnp.float32)
        weighted = jnp.einsum("hgqk,khd->qhgd", rounded, all_values)
        result = weighted / jnp.transpose(row_total, (2, 0, 1))[..., None]
        return result.astype(jnp.bfloat16).reshape(N_PAIR, 2, BLK, QH * HD)

    return lax.map(per_request, jnp.arange(REQUESTS, dtype=jnp.int32))
```

```python
import functools

import jax
import jax.numpy as jnp
from jax import lax
from jax.experimental import pallas as pl
from jax.experimental.pallas import tpu as pltpu
from jax.sharding import PartitionSpec as P

QH = 64
KVH = 8
HD = 128
GROUP = QH // KVH
PAGE = 8
PAGES_DEV = 64
SLOTS = 128
CHUNKS = 8
PER_CHUNK = SLOTS // CHUNKS
ROWS = 16
LANES = 512
Z_ORDER = (1, 7, 2, 6, 3, 5, 4, 0)
MESH = pl.DeviceIdType.MESH


def shifted(me, dy, dz, dx, dc):
    yh, z, x, c = me // 64, me // 8 % 8, me // 2 % 4, me % 2
    return (((yh + dy) % 2 * 8 + (z + dz) % 8) * 4 + (x + dx) % 4) * 2 + (c + dc) % 2


def slot_steps():
    d = jnp.arange(SLOTS, dtype=jnp.int32)
    dz = jnp.tile(jnp.repeat(jnp.array(Z_ORDER, jnp.int32), 2), CHUNKS)
    return d // 64, dz, d // 16 % 4, d % 2


def tables(leaf_parent, node_pages, page_slot, request_leaf, prefix_len, me):
    dy, dz, dx, dc = slot_steps()
    order = jnp.arange(page_slot.shape[1], dtype=jnp.int32)[None, :]
    held = (page_slot // PAGES_DEV == me) & (order < node_pages[:, None])
    row_of = jnp.max(jnp.where(held, page_slot % PAGES_DEV, -1), axis=1)
    target = shifted(me, dy, dz, dx, dc)
    leaf_t = request_leaf[target]
    mid_t = leaf_parent[leaf_t]
    send_row = jnp.maximum(jnp.maximum(row_of[0], row_of[1 + mid_t]), jnp.maximum(row_of[17 + leaf_t], 0))
    leaf = request_leaf[me]
    mid = leaf_parent[leaf]
    nodes = jnp.stack([jnp.zeros_like(mid), 1 + mid, 17 + leaf])
    counts = node_pages[nodes]
    first = jnp.cumsum(counts) - counts
    rows = page_slot[nodes]
    seen = jnp.clip(prefix_len[me] - PAGE * (first[:, None] + order), 0, PAGE)
    seen = jnp.where(order < counts[:, None], seen, 0)
    holder = shifted(me, -dy, -dz, -dx, -dc)
    match = (rows // PAGES_DEV).reshape(-1)[:, None] == holder[None, :]
    seen_slot = jnp.sum(jnp.where(match, seen.reshape(-1)[:, None], 0), axis=0)
    return send_row, seen_slot


def exchange(rows_ref, pk_ref, pv_ref, sk_ref, sv_ref, buf, other, send, sems, send_sem, recv_sem, fwd_send, fwd_recv, suf_send, suf_recv, near):
    me = lax.axis_index("store")
    p = lax.axis_index("pair")
    barrier = pltpu.get_barrier_semaphore()
    plane = [(dy, dx, dc) for dy in range(2) for dx in range(4) for dc in range(2) if (dy, dx, dc) != (0, 0, 0)]
    for dz in range(1, 8):
        pl.semaphore_signal(barrier, inc=1, device_id=(shifted(me, 0, dz, 0, 0), p), device_id_type=MESH)
    for dy, dx, dc in plane:
        pl.semaphore_signal(barrier, inc=1, device_id=(shifted(me, dy, 0, dx, dc), (p + dy) % 2), device_id_type=MESH)
    pl.semaphore_signal(barrier, inc=1, device_id=(me, 1 - p), device_id_type=MESH)

    def pack(page_ref):
        def body(d, _):
            page = page_ref[rows_ref[d]]
            start = pl.multiple_of(d * ROWS, ROWS)
            send[pl.ds(start, ROWS), :] = jnp.concatenate([page[:, :LANES], page[:, LANES:]], axis=0)
            return 0
        lax.fori_loop(0, SLOTS, body, 0)

    @pl.when(p == 0)
    def _():
        pack(pk_ref)

    @pl.when(p == 1)
    def _():
        pack(pv_ref)

    pl.semaphore_wait(barrier, 8 + len(plane))
    for dy, dx, dc in plane:
        pl.semaphore_signal(near, inc=1, device_id=(shifted(me, dy, 0, dx, dc), (p + dy) % 2), device_id_type=MESH)
    pl.semaphore_wait(near, len(plane))

    def suffix(i, ref):
        return pltpu.make_async_remote_copy(ref, other.at[i], suf_send.at[i], suf_recv.at[i], device_id=(me, 1 - p), device_id_type=MESH)

    suffix(0, sk_ref).start()
    suffix(1, sv_ref).start()
    self_copy = pltpu.make_async_copy(send.at[pl.ds(14 * ROWS, ROWS)], buf.at[p, pl.ds(14 * ROWS, ROWS)], sems)
    self_copy.start()

    def send_chunk(g, _):
        dy, dx = g // 4, g % 4
        for iz, dz in enumerate(Z_ORDER):
            for dc in range(2):
                start = pl.multiple_of(g * PER_CHUNK * ROWS, PER_CHUNK * ROWS) + (iz * 2 + dc) * ROWS
                start = pl.multiple_of(start, ROWS)
                copy = pltpu.make_async_remote_copy(
                    send.at[pl.ds(start, ROWS)], buf.at[p, pl.ds(start, ROWS)], send_sem, recv_sem.at[g],
                    device_id=(shifted(me, dy, dz, dx, dc), (p + dy) % 2), device_id_type=MESH)
                if dz == 0 and dc == 0:
                    pl.when(g != 0)(copy.start)
                else:
                    copy.start()
        return 0

    lax.fori_loop(0, CHUNKS, send_chunk, 0)

    def chunk_rows(g):
        return pl.ds(pl.multiple_of(g * PER_CHUNK * ROWS, PER_CHUNK * ROWS), PER_CHUNK * ROWS)

    def forward(g):
        q = (p + g // 4) % 2
        return pltpu.make_async_remote_copy(buf.at[q, chunk_rows(g)], buf.at[q, chunk_rows(g)], fwd_send.at[g], fwd_recv.at[g],
                                            device_id=(me, 1 - p), device_id_type=MESH)

    def arrived(n, sem):
        part = send.at[pl.ds(0, n * ROWS)]
        pltpu.make_async_copy(part, part, sem).wait()

    def pass_on(g, _):
        @pl.when(g == 0)
        def _():
            arrived(PER_CHUNK - 1, recv_sem.at[0])
            self_copy.wait()

        @pl.when(g != 0)
        def _():
            arrived(PER_CHUNK, recv_sem.at[g])
        forward(g).start()
        return 0

    lax.fori_loop(0, CHUNKS, pass_on, 0)

    def finish(g, _):
        forward(g).wait_send()
        arrived(PER_CHUNK, fwd_recv.at[g])
        return 0

    lax.fori_loop(0, CHUNKS, finish, 0)
    suffix(0, sk_ref).wait()
    suffix(1, sv_ref).wait()
    arrived(SLOTS - 1, send_sem)


def attend_block(state, head_queries, block_keys, block_values, allowed, score_scale):
    running_max, running_sum, weighted = state
    scores = jnp.einsum("hqd,khd->hqk", head_queries, block_keys, preferred_element_type=jnp.float32) * score_scale
    scores = jnp.where(allowed, scores, -1e30)
    new_max = jnp.maximum(running_max, jnp.max(scores, axis=-1))
    factor = jnp.exp(running_max - new_max)
    weights = jnp.exp(scores - new_max[..., None])
    running_sum = running_sum * factor + jnp.sum(weights, axis=-1)
    weighted = weighted * factor[..., None] + jnp.einsum(
        "hqk,khd->hqd", weights.astype(jnp.bfloat16), block_values, preferred_element_type=jnp.float32)
    return new_max, running_sum, weighted


def mirror_pos(pair_index):
    block_ids = jnp.stack([pair_index, 3 - pair_index])
    return (block_ids[:, None] * 128 + jnp.arange(128, dtype=jnp.int32)[None, :]).reshape(-1)


def local(queries, suffix_keys, suffix_values, page_keys, page_values, leaf_parent, node_pages, page_slot, request_leaf, prefix_len):
    me = lax.axis_index("store")
    p = lax.axis_index("pair")
    send_row, seen_slot = tables(leaf_parent, node_pages, page_slot, request_leaf, prefix_len, me)
    sk = suffix_keys.reshape(256, KVH * HD)
    sv = suffix_values.reshape(256, KVH * HD)
    vmem = pl.BlockSpec(memory_space=pltpu.VMEM)
    buf, other = pl.pallas_call(
        exchange,
        out_shape=(jax.ShapeDtypeStruct((2, SLOTS * ROWS, LANES), jnp.bfloat16), jax.ShapeDtypeStruct((2, 256, 1024), jnp.bfloat16)),
        in_specs=[pl.BlockSpec(memory_space=pltpu.SMEM)] + [vmem] * 4,
        out_specs=(vmem, vmem),
        scratch_shapes=[pltpu.VMEM((SLOTS * ROWS, LANES), jnp.bfloat16), pltpu.SemaphoreType.DMA, pltpu.SemaphoreType.DMA,
                        pltpu.SemaphoreType.DMA((CHUNKS,)), pltpu.SemaphoreType.DMA((CHUNKS,)), pltpu.SemaphoreType.DMA((CHUNKS,)),
                        pltpu.SemaphoreType.DMA((2,)), pltpu.SemaphoreType.DMA((2,)), pltpu.SemaphoreType.REGULAR],
        compiler_params=pltpu.CompilerParams(collective_id=1, has_side_effects=True, vmem_limit_bytes=48 * 2**20),
    )(send_row, page_keys, page_values, sk, sv)
    pages = buf.reshape(2, SLOTS, 2, PAGE, 4, HD).transpose(0, 1, 3, 2, 4, 5).reshape(2, SLOTS * PAGE, KVH, HD)
    usable = (jnp.arange(PAGE, dtype=jnp.int32)[None, :] < seen_slot[:, None]).reshape(1, 1, -1)
    scale = HD ** -0.5
    q = jnp.transpose(queries.reshape(256, KVH, GROUP, HD), (1, 0, 2, 3)).reshape(KVH, 256 * GROUP, HD)
    state = (jnp.full((KVH, 2048), -1e30, jnp.float32), jnp.zeros((KVH, 2048), jnp.float32), jnp.zeros((KVH, 2048, HD), jnp.float32))
    qp, op = mirror_pos(p), mirror_pos(1 - p)
    own = jnp.repeat(qp[:, None] >= qp[None, :], GROUP, axis=0)[None]
    theirs = jnp.repeat(qp[:, None] >= op[None, :], GROUP, axis=0)[None]
    state = attend_block(state, q, sk.reshape(-1, KVH, HD), sv.reshape(-1, KVH, HD), own, scale)
    state = attend_block(state, q, other[0].reshape(-1, KVH, HD), other[1].reshape(-1, KVH, HD), theirs, scale)
    for b in range(4):
        s = slice(b * 256, b * 256 + 256)
        state = attend_block(state, q, pages[0, s], pages[1, s], usable[:, :, s], scale)
    _, total, weighted = state
    result = (weighted / total[..., None]).reshape(KVH, 256, GROUP, HD)
    return jnp.transpose(result, (1, 0, 2, 3)).astype(jnp.bfloat16).reshape(queries.shape)


def solution(mesh):
    big = P("store", "pair", None, None, None)
    return jax.shard_map(
        local, mesh=mesh,
        in_specs=(big, big, big, P("store", None, None), P("store", None, None), P(), P(), P(), P(), P()),
        out_specs=big, check_vma=False)
```

```python
import jax
import jax.numpy as jnp
from jax import lax
from jax.experimental import pallas as pl
from jax.experimental.pallas import tpu as pltpu
from jax.sharding import PartitionSpec as P

QH = 64
KVH = 8
HD = 128
GROUP = QH // KVH
BLK = 128
LOCAL = 2 * BLK
PAGE = 8
PAGES_DEV = 64
MIDS = 16
SLOTS = 128
CHUNKS = 8
PER_CHUNK = SLOTS // CHUNKS
CHUNK_KEYS = PER_CHUNK * PAGE
ROWS = 16
LANES = 512
CHUNK_ROWS = PER_CHUNK * ROWS
STEP_KEYS = 256
DIRECT = (6, 7)
FIRST_DIRECT = DIRECT[0]
Z_ORDER = (1, 0, 2, 7, 3, 6, 4, 5)
SELF_ITEM = 2
SCALE = HD ** -0.5 * 1.4426950408889634
HIDDEN = -1e30
MESH = pl.DeviceIdType.MESH


def shifted(me, dy, dz, dx, dc):
    yh, z, x, c = me // 64, me // 8 % 8, me // 2 % 4, me % 2
    return (((yh + dy) % 2 * 8 + (z + dz) % 8) * 4 + (x + dx) % 4) * 2 + (c + dc) % 2


def chunk_step(g):
    return g % 2, g // 2


def score(q, keys):
    return lax.dot_general(q, keys, (((1,), (1,)), ((), ())), preferred_element_type=jnp.float32)


def load(h, rows, state):
    return tuple(ref[h, rows] for ref in state)


def attend(scores, values, before, bias=None, causal=False):
    scores = scores * SCALE
    if bias is not None:
        scores = scores + bias
    if causal:
        shape = scores.shape
        ordered = lax.broadcasted_iota(jnp.int32, shape, 0) >= lax.broadcasted_iota(jnp.int32, shape, 1)
        scores = jnp.where(ordered, scores, HIDDEN)
    top = jnp.max(scores, axis=1, keepdims=True)
    if before is None:
        new_max = jnp.broadcast_to(top, (scores.shape[0], HD))
    else:
        old_out, old_max, old_total = before
        new_max = jnp.maximum(old_max, top)
        factor = jnp.exp2(old_max - new_max)
    parts = [jnp.exp2(scores[:, j * 128:j * 128 + 128] - new_max) for j in range(scores.shape[1] // 128)]
    total = parts[0]
    for part in parts[1:]:
        total = total + part
    weights = [part.astype(jnp.bfloat16) for part in parts]
    weights = jnp.concatenate(weights, axis=1) if len(parts) > 1 else weights[0]
    out = jnp.dot(weights, values, preferred_element_type=jnp.float32)
    if before is not None:
        total = total + old_total * factor
        out = out + old_out * factor
    return out, new_max, total


def group_heads(k, q_ref, rows, keys, values, state, finish, first=False, **mask):
    scores, before = [None] * GROUP, [None] * GROUP
    for g in range(GROUP + AHEAD):
        if g < GROUP:
            h = k * GROUP + g
            scores[g] = score(q_ref[rows, head_columns(h)], keys)
            before[g] = None if first else load(h, rows, state)
        if g >= AHEAD:
            done = g - AHEAD
            finish(k * GROUP + done, attend(scores[done], values, before[done], **mask))


AHEAD = 8


def keep(h, rows, state, result):
    for ref, value in zip(state, result):
        ref[h, rows] = value


def head_columns(h):
    return pl.ds(pl.multiple_of(h * HD, HD), HD)


def suffix_own(q_ref, suf, state):
    rows = pl.ds(0, LOCAL)

    def body(k, _):
        keys, values = suf[0, :, head_columns(k)], suf[1, :, head_columns(k)]
        group_heads(k, q_ref, rows, keys, values, state, lambda h, r: keep(h, rows, state, r), first=True, causal=True)
        return 0
    lax.fori_loop(0, KVH, body, 0)


def suffix_other(q_ref, other, state, p):
    def run(rows, key_count):
        def body(k, _):
            keys, values = other[0, pl.ds(0, key_count), head_columns(k)], other[1, pl.ds(0, key_count), head_columns(k)]
            group_heads(k, q_ref, rows, keys, values, state, lambda h, r: keep(h, rows, state, r))
            return 0
        lax.fori_loop(0, KVH, body, 0)

    @pl.when(p == 0)
    def _():
        run(pl.ds(BLK, BLK), LOCAL)

    @pl.when(p == 1)
    def _():
        run(pl.ds(0, LOCAL), BLK)


def prefix_step(s, q_ref, paged, bias_ref, state):
    rows, span = pl.ds(0, LOCAL), pl.ds(s * STEP_KEYS, STEP_KEYS)

    def body(k, _):
        group_heads(k, q_ref, rows, paged[0, k, span], paged[1, k, span], state,
                    lambda h, r: keep(h, rows, state, r), bias=bias_ref[pl.ds(0, 1), span])
        return 0
    lax.fori_loop(0, KVH, body, 0)


def last_step(s, q_ref, paged, bias_ref, state, out_ref, out_sem):
    rows, span = pl.ds(0, LOCAL), pl.ds(s * STEP_KEYS, STEP_KEYS)

    def out_copy(k):
        columns = pl.ds(pl.multiple_of(k * GROUP * HD, GROUP * HD), GROUP * HD)
        return pltpu.make_async_copy(q_ref.at[:, columns], out_ref.at[:, columns], out_sem.at[k])

    def divide(h, result):
        out, _, total = result
        total = jnp.sum(total, axis=1, keepdims=True)
        q_ref[:, head_columns(h)] = (out / total).astype(jnp.bfloat16)

    def body(k, _):
        group_heads(k, q_ref, rows, paged[0, k, span], paged[1, k, span], state, divide, bias=bias_ref[pl.ds(0, 1), span])
        out_copy(k).start()
        return 0
    lax.fori_loop(0, KVH, body, 0)

    def finish(k, _):
        out_copy(k).wait()
        return 0
    lax.fori_loop(0, KVH, finish, 0)


def unfold(g, land, paged):
    for i in range(2):
        for lane in range(4):
            block = land[i, pl.ds(g * CHUNK_ROWS, CHUNK_ROWS), lane * HD:(lane + 1) * HD]
            block = block.astype(jnp.float32).reshape(PER_CHUNK, 2, PAGE, HD)
            for half in range(2):
                part = block[:, half].reshape(CHUNK_KEYS, HD).astype(jnp.bfloat16)
                paged[i, half * 4 + lane, pl.ds(g * CHUNK_KEYS, CHUNK_KEYS)] = part


def visible_bias(me, parent_ref, pages_ref, leaf_ref, length_ref, slot_ref, bias_ref):
    leaf = leaf_ref[me]
    mid = parent_ref[leaf]
    length = length_ref[me]
    width = slot_ref.shape[1]
    key = lax.broadcasted_iota(jnp.int32, (1, SLOTS * PAGE), 1)
    d = key // PAGE
    g, item = d // PER_CHUNK, d % PER_CHUNK
    iz, dc = item // 2, item % 2
    dz = jnp.where(iz % 2 == 0, iz // 2 + 1, (8 - iz // 2) % 8)
    dy, dx = chunk_step(g)
    holder = shifted(me + jnp.zeros_like(key), 2 - dy, 8 - dz, 4 - dx, 2 - dc).astype(jnp.float32)
    across = lax.broadcasted_iota(jnp.int32, (width, width), 1)
    down = lax.broadcasted_iota(jnp.int32, (width, width), 0)
    order = lax.broadcasted_iota(jnp.int32, (width, 1), 0)
    seen = jnp.zeros(key.shape, jnp.float32)
    first = 0
    for node in (0, 1 + mid, 1 + MIDS + leaf):
        count = pages_ref[node]
        row = (slot_ref[pl.ds(node, 1), :] // PAGES_DEV).astype(jnp.float32)
        column = jnp.sum(jnp.where(across == down, jnp.broadcast_to(row, (width, width)), 0.0), axis=1, keepdims=True)
        tokens = jnp.clip(length - PAGE * (first + order), 0, PAGE)
        tokens = jnp.where(order < count, tokens, 0).astype(jnp.float32)
        match = column == holder
        seen = seen + jnp.sum(jnp.where(match, tokens, 0.0), axis=0, keepdims=True)
        first = first + count
    shown = (key % PAGE).astype(jnp.float32) < seen
    bias_ref[...] = jnp.broadcast_to(jnp.where(shown, 0.0, HIDDEN), bias_ref.shape)


def kernel(parent_ref, pages_ref, leaf_ref, length_ref, slot_ref, pk_ref, pv_ref, q_hbm, sk_hbm, sv_hbm, out_ref,
           q_ref, suf, other, land, send, paged, acc_ref, max_ref, sum_ref, bias_ref, row_vec, row_smem,
           load_sem, row_sem, self_sem, send_sem, recv_sem, fwd_send, fwd_recv, suf_send, suf_recv, out_sem, near):
    me = lax.axis_index("store")
    p = lax.axis_index("pair")
    state = (acc_ref, max_ref, sum_ref)
    barrier = pltpu.get_barrier_semaphore()
    plane = [(dy, dx, dc) for dy in range(2) for dx in range(4) for dc in range(2) if (dy, dx, dc) != (0, 0, 0)]

    def tell(sem, dy, dz, dx, dc):
        pl.semaphore_signal(sem, inc=1, device_id=(shifted(me, dy, dz, dx, dc), (p + dy) % 2), device_id_type=MESH)

    for dy, dx, dc in plane:
        tell(barrier, dy, 0, dx, dc)
    for dz in range(1, 8):
        tell(barrier, 0, dz, 0, 0)
    pl.semaphore_signal(barrier, inc=1, device_id=(me, 1 - p), device_id_type=MESH)

    loads = [pltpu.make_async_copy(sk_hbm, suf.at[0], load_sem.at[0]),
             pltpu.make_async_copy(sv_hbm, suf.at[1], load_sem.at[1]),
             pltpu.make_async_copy(q_hbm, q_ref, load_sem.at[2])]
    for copy in loads:
        copy.start()

    places = slot_ref[...]
    mine = jnp.where(places // PAGES_DEV == me, places % PAGES_DEV, 0)
    best = jnp.max(mine, axis=1, keepdims=True)
    row_vec[...] = jnp.broadcast_to(best, row_vec.shape)
    to_smem = pltpu.make_async_copy(row_vec, row_smem, row_sem)
    to_smem.start()
    to_smem.wait()

    def target(g, item):
        dy, dx = chunk_step(g)
        return dy, Z_ORDER[item // 2], dx, item % 2

    def pack(g, _):
        for item in range(PER_CHUNK):
            dy, dz, dx, dc = target(g, item)
            leaf = leaf_ref[shifted(me, dy, dz, dx, dc)]
            mid = parent_ref[leaf]
            row = jnp.maximum(jnp.maximum(row_smem[0, 0], row_smem[1 + mid, 0]), row_smem[1 + MIDS + leaf, 0])
            start = pl.multiple_of(g * CHUNK_ROWS + item * ROWS, ROWS)

            def put(i, page_ref):
                page = page_ref[jnp.clip(row, 0, PAGES_DEV - 1)]
                send[i, pl.ds(start, ROWS), :] = jnp.concatenate([page[:, :LANES], page[:, LANES:]], axis=0)

            @pl.when((p == 0) | (g >= FIRST_DIRECT))
            def _():
                put(0, pk_ref)

            @pl.when((p == 1) | (g >= FIRST_DIRECT))
            def _():
                put(1, pv_ref)
        return 0

    def chunk_span(g):
        return pl.ds(pl.multiple_of(g * CHUNK_ROWS, CHUNK_ROWS), CHUNK_ROWS)

    def own_item(g):
        span = pl.ds(SELF_ITEM * ROWS, ROWS)
        return pltpu.make_async_copy(send.at[p, span], land.at[p, span], self_sem)

    def send_chunk(g, i, extra=0):
        for item in range(PER_CHUNK):
            dy, dz, dx, dc = target(g, item)
            span = pl.ds(pl.multiple_of(g * CHUNK_ROWS + item * ROWS, ROWS), ROWS)
            copy = pltpu.make_async_remote_copy(
                send.at[i, span], land.at[i, span], send_sem.at[extra], recv_sem.at[g],
                device_id=(shifted(me, dy, dz, dx, dc), (p + dy) % 2), device_id_type=MESH)
            if item == SELF_ITEM:
                pl.when(g != 0)(copy.start)
            else:
                copy.start()

    lax.fori_loop(0, 2, pack, 0)
    pl.semaphore_wait(barrier, 8 + len(plane))
    for dy, dx, dc in plane:
        tell(near, dy, 0, dx, dc)
    loads[0].wait()
    loads[1].wait()

    def suffix_copy(i, rows):
        return pltpu.make_async_remote_copy(suf.at[i, pl.ds(0, rows)], other.at[i, pl.ds(0, rows)], suf_send.at[i], suf_recv.at[i],
                                            device_id=(me, 1 - p), device_id_type=MESH)

    for rows, who in ((BLK, 0), (LOCAL, 1)):
        @pl.when(p == who)
        def _():
            suffix_copy(0, rows).start()
            suffix_copy(1, rows).start()
    pl.semaphore_wait(near, len(plane))
    own_item(0).start()

    def pack_send(g, _):
        @pl.when(g >= 2)
        def _():
            pack(g, 0)

        send_chunk(g, p)

        @pl.when(g >= FIRST_DIRECT)
        def _():
            send_chunk(g, 1 - p, 1)
        return 0

    lax.fori_loop(0, CHUNKS, pack_send, 0)

    def forward(g):
        q = (p + g % 2) % 2
        part = land.at[q, chunk_span(g)]
        return pltpu.make_async_remote_copy(part, part, fwd_send.at[g], fwd_recv.at[g], device_id=(me, 1 - p), device_id_type=MESH)

    def arrived(items, sem):
        part = send.at[0, pl.ds(0, items * ROWS)]
        pltpu.make_async_copy(part, part, sem).wait()

    def receive(g):
        if g in DIRECT:
            arrived(2 * PER_CHUNK, recv_sem.at[g])
            return
        arrived(PER_CHUNK - (g == 0), recv_sem.at[g])
        if g == 0:
            own_item(0).wait()
        forward(g).start()

    def whole(g):
        if g not in DIRECT:
            arrived(PER_CHUNK, fwd_recv.at[g])
        unfold(g, land, paged)

    visible_bias(me, parent_ref, pages_ref, leaf_ref, length_ref, slot_ref, bias_ref)
    loads[2].wait()
    suffix_own(q_ref, suf, state)
    receive(0)
    receive(1)
    for rows, who in ((LOCAL, 0), (BLK, 1)):
        @pl.when(p == who)
        def _():
            for i in range(2):
                pltpu.make_async_copy(suf.at[i, pl.ds(0, rows)], suf.at[i, pl.ds(0, rows)], suf_recv.at[i]).wait()
    suffix_other(q_ref, other, state, p)
    receive(2)
    whole(0)
    receive(3)
    whole(1)
    prefix_step(0, q_ref, paged, bias_ref, state)
    receive(4)
    whole(2)
    receive(5)
    whole(3)
    prefix_step(1, q_ref, paged, bias_ref, state)
    whole(4)
    whole(5)
    prefix_step(2, q_ref, paged, bias_ref, state)
    receive(6)
    whole(6)
    receive(7)
    whole(7)
    last_step(3, q_ref, paged, bias_ref, state, out_ref, out_sem)

    for g in range(CHUNKS):
        if g not in DIRECT:
            forward(g).wait_send()
    for rows, who in ((BLK, 0), (LOCAL, 1)):
        @pl.when(p == who)
        def _():
            suffix_copy(0, rows).wait_send()
            suffix_copy(1, rows).wait_send()
    arrived(SLOTS - 1, send_sem.at[0])
    arrived(len(DIRECT) * PER_CHUNK, send_sem.at[1])


def local(queries, suffix_keys, suffix_values, page_keys, page_values, leaf_parent, node_pages, page_slot, request_leaf, prefix_len):
    vmem = pl.BlockSpec(memory_space=pltpu.VMEM)
    smem = pl.BlockSpec(memory_space=pltpu.SMEM)
    anywhere = pl.BlockSpec(memory_space=pl.ANY)
    bf16, f32 = jnp.bfloat16, jnp.float32
    dma = pltpu.SemaphoreType.DMA
    nodes = page_slot.shape[0]
    out = pl.pallas_call(
        kernel,
        out_shape=jax.ShapeDtypeStruct((LOCAL, QH * HD), bf16),
        in_specs=[smem] * 4 + [vmem] * 3 + [anywhere] * 3,
        out_specs=anywhere,
        scratch_shapes=[
            pltpu.VMEM((LOCAL, QH * HD), bf16),
            pltpu.VMEM((2, LOCAL, KVH * HD), bf16),
            pltpu.VMEM((2, LOCAL, KVH * HD), bf16),
            pltpu.VMEM((2, SLOTS * ROWS, LANES), bf16),
            pltpu.VMEM((2, SLOTS * ROWS, LANES), bf16),
            pltpu.VMEM((2, KVH, SLOTS * PAGE, HD), bf16),
            pltpu.VMEM((QH, LOCAL, HD), f32),
            pltpu.VMEM((QH, LOCAL, HD), f32),
            pltpu.VMEM((QH, LOCAL, HD), f32),
            pltpu.VMEM((8, SLOTS * PAGE), f32),
            pltpu.VMEM((nodes, 128), jnp.int32),
            pltpu.SMEM((nodes, 128), jnp.int32),
            dma((3,)), dma, dma, dma((2,)), dma((CHUNKS,)), dma((CHUNKS,)), dma((CHUNKS,)), dma((2,)), dma((2,)), dma((KVH,)),
            pltpu.SemaphoreType.REGULAR,
        ],
        compiler_params=pltpu.CompilerParams(collective_id=1, has_side_effects=True, vmem_limit_bytes=60 * 2**20),
    )(leaf_parent, node_pages, request_leaf, prefix_len, page_slot, page_keys, page_values,
      queries.reshape(LOCAL, QH * HD), suffix_keys.reshape(LOCAL, KVH * HD), suffix_values.reshape(LOCAL, KVH * HD))
    return out.reshape(queries.shape)


def solution(mesh):
    big = P("store", "pair", None, None, None)
    return jax.shard_map(
        local, mesh=mesh,
        in_specs=(big, big, big, P("store", None, None), P("store", None, None), P(), P(), P(), P(), P()),
        out_specs=big, check_vma=False)
```

```python
import jax
import jax.numpy as jnp
from jax import lax
from jax.experimental import pallas as pl
from jax.experimental.pallas import tpu as pltpu
from jax.sharding import PartitionSpec as P

QH = 64
KVH = 8
HD = 128
GROUP = QH // KVH
BLK = 128
LOCAL = 2 * BLK
PAGE = 8
PAGES_DEV = 64
MIDS = 16
SLOTS = 128
CHUNKS = 8
PER_CHUNK = SLOTS // CHUNKS
CHUNK_KEYS = PER_CHUNK * PAGE
ROWS = 16
LANES = 512
CHUNK_ROWS = PER_CHUNK * ROWS
DIRECT = (6, 7)
FIRST_DIRECT = DIRECT[0]
Z_ORDER = (1, 0, 2, 7, 3, 6, 4, 5)
SELF_ITEM = 2
SCALE = HD ** -0.5 * 1.4426950408889634
HIDDEN = -1e30
MESH = pl.DeviceIdType.MESH


def shifted(me, dy, dz, dx, dc):
    yh, z, x, c = me // 64, me // 8 % 8, me // 2 % 4, me % 2
    return (((yh + dy) % 2 * 8 + (z + dz) % 8) * 4 + (x + dx) % 4) * 2 + (c + dc) % 2


def chunk_step(g):
    return g % 2, g // 2


def score(q, keys):
    return lax.dot_general(q, keys, (((1,), (1,)), ((), ())), preferred_element_type=jnp.float32)


def load(h, rows, state):
    return tuple(ref[h, rows] for ref in state)


def attend(scores, values, before, bias=None, causal=False):
    scores = scores * SCALE
    if bias is not None:
        scores = scores + bias
    if causal:
        shape = scores.shape
        ordered = lax.broadcasted_iota(jnp.int32, shape, 0) >= lax.broadcasted_iota(jnp.int32, shape, 1)
        scores = jnp.where(ordered, scores, HIDDEN)
    top = jnp.max(scores, axis=1, keepdims=True)
    if before is None:
        new_max = jnp.broadcast_to(top, (scores.shape[0], HD))
    else:
        old_out, old_max, old_total = before
        new_max = jnp.maximum(old_max, top)
        factor = jnp.exp2(old_max - new_max)
    parts = [jnp.exp2(scores[:, j * 128:j * 128 + 128] - new_max) for j in range(scores.shape[1] // 128)]
    total = parts[0]
    for part in parts[1:]:
        total = total + part
    weights = [part.astype(jnp.bfloat16) for part in parts]
    weights = jnp.concatenate(weights, axis=1) if len(parts) > 1 else weights[0]
    out = jnp.dot(weights, values, preferred_element_type=jnp.float32)
    if before is not None:
        total = total + old_total * factor
        out = out + old_out * factor
    return out, new_max, total


def group_heads(k, q_ref, rows, keys, values, state, finish, first=False, **mask):
    scores, before = [None] * GROUP, [None] * GROUP
    for g in range(GROUP + AHEAD):
        if g < GROUP:
            h = k * GROUP + g
            scores[g] = score(q_ref[rows, head_columns(h)], keys)
            before[g] = None if first else load(h, rows, state)
        if g >= AHEAD:
            done = g - AHEAD
            finish(k * GROUP + done, attend(scores[done], values, before[done], **mask))


AHEAD = 8


def keep(h, rows, state, result):
    for ref, value in zip(state, result):
        ref[h, rows] = value


def head_columns(h):
    return pl.ds(pl.multiple_of(h * HD, HD), HD)


def suffix_own(q_ref, suf, state):
    rows = pl.ds(0, LOCAL)

    def body(k, _):
        keys, values = suf[0, :, head_columns(k)], suf[1, :, head_columns(k)]
        group_heads(k, q_ref, rows, keys, values, state, lambda h, r: keep(h, rows, state, r), first=True, causal=True)
        return 0
    lax.fori_loop(0, KVH, body, 0)


def suffix_other(q_ref, other, state, p):
    def run(rows, key_count):
        def body(k, _):
            keys, values = other[0, pl.ds(0, key_count), head_columns(k)], other[1, pl.ds(0, key_count), head_columns(k)]
            group_heads(k, q_ref, rows, keys, values, state, lambda h, r: keep(h, rows, state, r))
            return 0
        lax.fori_loop(0, KVH, body, 0)

    @pl.when(p == 0)
    def _():
        run(pl.ds(BLK, BLK), LOCAL)

    @pl.when(p == 1)
    def _():
        run(pl.ds(0, LOCAL), BLK)


def prefix_step(start, count, q_ref, paged, bias_ref, state):
    rows, span = pl.ds(0, LOCAL), pl.ds(start * CHUNK_KEYS, count * CHUNK_KEYS)

    def body(k, _):
        group_heads(k, q_ref, rows, paged[0, k, span], paged[1, k, span], state,
                    lambda h, r: keep(h, rows, state, r), bias=bias_ref[pl.ds(0, 1), span])
        return 0
    lax.fori_loop(0, KVH, body, 0)


def out_copy(k, q_ref, out_ref, out_sem):
    columns = pl.ds(pl.multiple_of(k * GROUP * HD, GROUP * HD), GROUP * HD)
    return pltpu.make_async_copy(q_ref.at[:, columns], out_ref.at[:, columns], out_sem.at[k])


def last_step(part, start, count, q_ref, paged, bias_ref, state, out_ref, out_sem):
    rows, span = pl.ds(0, LOCAL), pl.ds(start * CHUNK_KEYS, count * CHUNK_KEYS)

    def divide(h, result):
        out, _, total = result
        total = jnp.sum(total, axis=1, keepdims=True)
        q_ref[:, head_columns(h)] = (out / total).astype(jnp.bfloat16)

    def body(k, _):
        group_heads(k, q_ref, rows, paged[0, k, span], paged[1, k, span], state, divide, bias=bias_ref[pl.ds(0, 1), span])
        out_copy(k, q_ref, out_ref, out_sem).start()
        return 0
    lax.fori_loop(part * KVH // 2, (part + 1) * KVH // 2, body, 0)


def unfold(g, land, paged):
    for i in range(2):
        for lane in range(4):
            block = land[i, pl.ds(g * CHUNK_ROWS, CHUNK_ROWS), lane * HD:(lane + 1) * HD]
            block = block.astype(jnp.float32).reshape(PER_CHUNK, 2, PAGE, HD)
            for half in range(2):
                part = block[:, half].reshape(CHUNK_KEYS, HD).astype(jnp.bfloat16)
                paged[i, half * 4 + lane, pl.ds(g * CHUNK_KEYS, CHUNK_KEYS)] = part


def unfold_direct(part, land, paged):
    for g in DIRECT:
        for lane in range(4):
            block = land[part, pl.ds(g * CHUNK_ROWS, CHUNK_ROWS), lane * HD:(lane + 1) * HD]
            block = block.astype(jnp.float32).reshape(PER_CHUNK, 2, PAGE, HD)
            for i in range(2):
                paged[i, part * 4 + lane, pl.ds(g * CHUNK_KEYS, CHUNK_KEYS)] = block[:, i].reshape(CHUNK_KEYS, HD).astype(jnp.bfloat16)


def visible_bias(me, parent_ref, pages_ref, leaf_ref, length_ref, slot_ref, bias_ref):
    leaf = leaf_ref[me]
    mid = parent_ref[leaf]
    length = length_ref[me]
    width = slot_ref.shape[1]
    key = lax.broadcasted_iota(jnp.int32, (1, SLOTS * PAGE), 1)
    d = key // PAGE
    g, item = d // PER_CHUNK, d % PER_CHUNK
    iz, dc = item // 2, item % 2
    dz = jnp.where(iz % 2 == 0, iz // 2 + 1, (8 - iz // 2) % 8)
    dy, dx = chunk_step(g)
    holder = shifted(me + jnp.zeros_like(key), 2 - dy, 8 - dz, 4 - dx, 2 - dc).astype(jnp.float32)
    across = lax.broadcasted_iota(jnp.int32, (width, width), 1)
    down = lax.broadcasted_iota(jnp.int32, (width, width), 0)
    order = lax.broadcasted_iota(jnp.int32, (width, 1), 0)
    seen = jnp.zeros(key.shape, jnp.float32)
    first = 0
    for node in (0, 1 + mid, 1 + MIDS + leaf):
        count = pages_ref[node]
        row = (slot_ref[pl.ds(node, 1), :] // PAGES_DEV).astype(jnp.float32)
        column = jnp.sum(jnp.where(across == down, jnp.broadcast_to(row, (width, width)), 0.0), axis=1, keepdims=True)
        tokens = jnp.clip(length - PAGE * (first + order), 0, PAGE)
        tokens = jnp.where(order < count, tokens, 0).astype(jnp.float32)
        match = column == holder
        seen = seen + jnp.sum(jnp.where(match, tokens, 0.0), axis=0, keepdims=True)
        first = first + count
    shown = (key % PAGE).astype(jnp.float32) < seen
    bias_ref[...] = jnp.broadcast_to(jnp.where(shown, 0.0, HIDDEN), bias_ref.shape)


def kernel(parent_ref, pages_ref, leaf_ref, length_ref, slot_hbm, pk_ref, pv_ref, q_hbm, sk_hbm, sv_hbm, out_ref,
           slot_ref, q_ref, suf, other, land, send, paged, acc_ref, max_ref, sum_ref, bias_ref, row_vec, row_smem,
           load_sem, row_sem, self_sem, send_sem, recv_sem, fwd_send, fwd_recv, suf_send, suf_recv, out_sem, near):
    me = lax.axis_index("store")
    p = lax.axis_index("pair")
    state = (acc_ref, max_ref, sum_ref)
    barrier = pltpu.get_barrier_semaphore()
    plane = [(dy, dx, dc) for dy in range(2) for dx in range(4) for dc in range(2) if (dy, dx, dc) != (0, 0, 0)]

    def tell(sem, dy, dz, dx, dc):
        pl.semaphore_signal(sem, inc=1, device_id=(shifted(me, dy, dz, dx, dc), (p + dy) % 2), device_id_type=MESH)

    load_slots = pltpu.make_async_copy(slot_hbm, slot_ref, row_sem)
    load_slots.start()
    for dy, dx, dc in plane:
        tell(barrier, dy, 0, dx, dc)
    for dz in range(1, 8):
        tell(barrier, 0, dz, 0, 0)
    pl.semaphore_signal(barrier, inc=1, device_id=(me, 1 - p), device_id_type=MESH)

    loads = [pltpu.make_async_copy(sk_hbm, suf.at[0], load_sem.at[0]),
             pltpu.make_async_copy(sv_hbm, suf.at[1], load_sem.at[1]),
             pltpu.make_async_copy(q_hbm, q_ref, load_sem.at[2])]
    for copy in loads:
        copy.start()

    load_slots.wait()
    places = slot_ref[...]
    mine = jnp.where(places // PAGES_DEV == me, places % PAGES_DEV, 0)
    best = jnp.max(mine, axis=1, keepdims=True)
    shape = (places.shape[0], 128)
    own_lane = lax.broadcasted_iota(jnp.int32, shape, 0) == lax.broadcasted_iota(jnp.int32, shape, 1)
    row_vec[...] = jnp.broadcast_to(jnp.sum(jnp.where(own_lane, best, 0), axis=0, keepdims=True), row_vec.shape)
    to_smem = pltpu.make_async_copy(row_vec, row_smem, row_sem)
    to_smem.start()
    to_smem.wait()

    def target(g, item):
        dy, dx = chunk_step(g)
        return dy, Z_ORDER[item // 2], dx, item % 2

    def pack(g, direct=False):
        for item in range(PER_CHUNK):
            dy, dz, dx, dc = target(g, item)
            leaf = leaf_ref[shifted(me, dy, dz, dx, dc)]
            mid = parent_ref[leaf]
            row = jnp.maximum(jnp.maximum(row_smem[0, 0], row_smem[0, 1 + mid]), row_smem[0, 1 + MIDS + leaf])
            start = pl.multiple_of(g * CHUNK_ROWS + item * ROWS, ROWS)

            row = jnp.clip(row, 0, PAGES_DEV - 1)

            def put(i, upper, lower):
                send[i, pl.ds(start, ROWS), :] = jnp.concatenate([upper, lower], axis=0)

            if direct:
                keys, values = pk_ref[row], pv_ref[row]
                put(0, keys[:, :LANES], values[:, :LANES])
                put(1, keys[:, LANES:], values[:, LANES:])
            else:
                @pl.when(p == 0)
                def _():
                    put(0, pk_ref[row][:, :LANES], pk_ref[row][:, LANES:])

                @pl.when(p == 1)
                def _():
                    put(1, pv_ref[row][:, :LANES], pv_ref[row][:, LANES:])

    def chunk_span(g):
        return pl.ds(pl.multiple_of(g * CHUNK_ROWS, CHUNK_ROWS), CHUNK_ROWS)

    def own_item(g):
        span = pl.ds(SELF_ITEM * ROWS, ROWS)
        return pltpu.make_async_copy(send.at[p, span], land.at[p, span], self_sem)

    def send_item(g, item, i, sem=None, extra=0):
        dy, dz, dx, dc = target(g, item)
        span = pl.ds(pl.multiple_of(g * CHUNK_ROWS + item * ROWS, ROWS), ROWS)
        pltpu.make_async_remote_copy(
            send.at[i, span], land.at[i, span], send_sem.at[extra], recv_sem.at[g if sem is None else sem],
            device_id=(shifted(me, dy, dz, dx, dc), (p + dy) % 2), device_id_type=MESH).start()

    def send_chunk(g, i, sem=None, extra=0):
        for item in range(PER_CHUNK):
            send_item(g, item, i, sem, extra)

    pack(0)
    pl.semaphore_wait(barrier, 8 + len(plane))
    for dy, dx, dc in plane:
        tell(near, dy, 0, dx, dc)
    for item in range(0, PER_CHUNK, 2):
        if item != SELF_ITEM:
            send_item(0, item, p)
    loads[0].wait()
    loads[1].wait()

    def suffix_copy(i, rows):
        return pltpu.make_async_remote_copy(suf.at[i, pl.ds(0, rows)], other.at[i, pl.ds(0, rows)], suf_send.at[i], suf_recv.at[i],
                                            device_id=(me, 1 - p), device_id_type=MESH)

    for rows, who in ((BLK, 0), (LOCAL, 1)):
        @pl.when(p == who)
        def _():
            suffix_copy(0, rows).start()
            suffix_copy(1, rows).start()
    own_item(0).start()
    pack(1)
    pl.semaphore_wait(near, len(plane))
    for item in range(1, PER_CHUNK, 2):
        send_item(0, item, p)
    send_chunk(1, p)

    def pack_send(g, _):
        pack(g)
        send_chunk(g, p)
        return 0

    def pack_send_lower(g, _):
        pack(g, direct=True)
        send_chunk(g, 0, DIRECT[0])
        return 0

    def send_upper(g, _):
        send_chunk(g, 1, DIRECT[1], 1)
        return 0

    lax.fori_loop(2, FIRST_DIRECT, pack_send, 0)
    lax.fori_loop(FIRST_DIRECT, CHUNKS, pack_send_lower, 0)
    lax.fori_loop(FIRST_DIRECT, CHUNKS, send_upper, 0)

    def forward(g):
        q = (p + g % 2) % 2
        part = land.at[q, chunk_span(g)]
        return pltpu.make_async_remote_copy(part, part, fwd_send.at[g], fwd_recv.at[g], device_id=(me, 1 - p), device_id_type=MESH)

    def arrived(items, sem):
        part = send.at[0, pl.ds(0, items * ROWS)]
        pltpu.make_async_copy(part, part, sem).wait()

    def receive(g):
        arrived(PER_CHUNK - (g == 0), recv_sem.at[g])
        if g == 0:
            own_item(0).wait()
        forward(g).start()

    def whole(g):
        arrived(PER_CHUNK, fwd_recv.at[g])
        unfold(g, land, paged)

    def direct_part(part):
        arrived(len(DIRECT) * PER_CHUNK, recv_sem.at[DIRECT[part]])
        unfold_direct(part, land, paged)

    visible_bias(me, parent_ref, pages_ref, leaf_ref, length_ref, slot_ref, bias_ref)
    loads[2].wait()
    suffix_own(q_ref, suf, state)
    receive(0)
    receive(1)
    for rows, who in ((LOCAL, 0), (BLK, 1)):
        @pl.when(p == who)
        def _():
            for i in range(2):
                pltpu.make_async_copy(suf.at[i, pl.ds(0, rows)], suf.at[i, pl.ds(0, rows)], suf_recv.at[i]).wait()
    suffix_other(q_ref, other, state, p)
    receive(2)
    whole(0)
    receive(3)
    whole(1)
    prefix_step(0, 2, q_ref, paged, bias_ref, state)
    receive(4)
    whole(2)
    receive(5)
    whole(3)
    prefix_step(2, 2, q_ref, paged, bias_ref, state)
    whole(4)
    whole(5)
    prefix_step(4, 2, q_ref, paged, bias_ref, state)
    for part in range(2):
        direct_part(part)
        last_step(part, 6, 2, q_ref, paged, bias_ref, state, out_ref, out_sem)
    for k in range(KVH):
        out_copy(k, q_ref, out_ref, out_sem).wait()

    for g in range(CHUNKS):
        if g not in DIRECT:
            forward(g).wait_send()
    for rows, who in ((BLK, 0), (LOCAL, 1)):
        @pl.when(p == who)
        def _():
            suffix_copy(0, rows).wait_send()
            suffix_copy(1, rows).wait_send()
    arrived(SLOTS - 1, send_sem.at[0])
    arrived(len(DIRECT) * PER_CHUNK, send_sem.at[1])


def local(queries, suffix_keys, suffix_values, page_keys, page_values, leaf_parent, node_pages, page_slot, request_leaf, prefix_len):
    vmem = pl.BlockSpec(memory_space=pltpu.VMEM)
    smem = pl.BlockSpec(memory_space=pltpu.SMEM)
    anywhere = pl.BlockSpec(memory_space=pl.ANY)
    bf16, f32 = jnp.bfloat16, jnp.float32
    dma = pltpu.SemaphoreType.DMA
    out = pl.pallas_call(
        kernel,
        out_shape=jax.ShapeDtypeStruct((LOCAL, QH * HD), bf16),
        in_specs=[smem] * 4 + [anywhere] + [vmem] * 2 + [anywhere] * 3,
        out_specs=anywhere,
        scratch_shapes=[
            pltpu.VMEM(page_slot.shape, jnp.int32),
            pltpu.VMEM((LOCAL, QH * HD), bf16),
            pltpu.VMEM((2, LOCAL, KVH * HD), bf16),
            pltpu.VMEM((2, LOCAL, KVH * HD), bf16),
            pltpu.VMEM((2, SLOTS * ROWS, LANES), bf16),
            pltpu.VMEM((2, SLOTS * ROWS, LANES), bf16),
            pltpu.VMEM((2, KVH, SLOTS * PAGE, HD), bf16),
            pltpu.VMEM((QH, LOCAL, HD), f32),
            pltpu.VMEM((QH, LOCAL, HD), f32),
            pltpu.VMEM((QH, LOCAL, HD), f32),
            pltpu.VMEM((8, SLOTS * PAGE), f32),
            pltpu.VMEM((8, 128), jnp.int32),
            pltpu.SMEM((8, 128), jnp.int32),
            dma((3,)), dma, dma, dma((2,)), dma((CHUNKS,)), dma((CHUNKS,)), dma((CHUNKS,)), dma((2,)), dma((2,)), dma((KVH,)),
            pltpu.SemaphoreType.REGULAR,
        ],
        compiler_params=pltpu.CompilerParams(collective_id=1, has_side_effects=True, vmem_limit_bytes=60 * 2**20),
    )(leaf_parent, node_pages, request_leaf, prefix_len, page_slot, page_keys, page_values,
      queries.reshape(LOCAL, QH * HD), suffix_keys.reshape(LOCAL, KVH * HD), suffix_values.reshape(LOCAL, KVH * HD))
    return out.reshape(queries.shape)


def solution(mesh):
    big = P("store", "pair", None, None, None)
    return jax.shard_map(
        local, mesh=mesh,
        in_specs=(big, big, big, P("store", None, None), P("store", None, None), P(), P(), P(), P(), P()),
        out_specs=big, check_vma=False)
```

```python
import jax
import jax.numpy as jnp
from jax import lax
from jax.experimental import pallas as pl
from jax.experimental.pallas import tpu as pltpu
from jax.sharding import PartitionSpec as P

QH = 64
KVH = 8
HD = 128
GROUP = QH // KVH
BLK = 128
LOCAL = 2 * BLK
PAGE = 8
PAGES_DEV = 64
MIDS = 16
SLOTS = 128
CHUNKS = 8
PER_CHUNK = SLOTS // CHUNKS
CHUNK_KEYS = PER_CHUNK * PAGE
ROWS = 16
LANES = 512
CHUNK_ROWS = PER_CHUNK * ROWS
DIRECT = (6, 7)
FIRST_DIRECT = DIRECT[0]
Z_ORDER = (1, 0, 2, 7, 3, 6, 4, 5)
SELF_ITEM = 2
SCALE = HD ** -0.5 * 1.4426950408889634
HIDDEN = -1e30
MESH = pl.DeviceIdType.MESH


def shifted(me, dy, dz, dx, dc):
    yh, z, x, c = (me >> 6) + dy, (me >> 3) + dz, (me >> 1) + dx, me + dc
    return ((yh & 1) << 6) + ((z & 7) << 3) + ((x & 3) << 1) + (c & 1)


def chunk_step(g):
    return g & 1, g >> 1


def score(q, keys):
    return lax.dot_general(q, keys, (((1,), (1,)), ((), ())), preferred_element_type=jnp.float32)


def load(h, rows, state):
    return tuple(ref[h, rows] for ref in state)


def attend(scores, values, before, bias=None, causal=False):
    scores = scores * SCALE
    if bias is not None:
        scores = scores + bias
    if causal:
        shape = scores.shape
        ordered = lax.broadcasted_iota(jnp.int32, shape, 0) >= lax.broadcasted_iota(jnp.int32, shape, 1)
        scores = jnp.where(ordered, scores, HIDDEN)
    top = jnp.max(scores, axis=1, keepdims=True)
    if before is None:
        new_max = jnp.broadcast_to(top, (scores.shape[0], HD))
    else:
        old_out, old_max, old_total = before
        new_max = jnp.maximum(old_max, top)
        factor = jnp.exp2(old_max - new_max)
    parts = [jnp.exp2(scores[:, j * 128:j * 128 + 128] - new_max) for j in range(scores.shape[1] // 128)]
    total = parts[0]
    for part in parts[1:]:
        total = total + part
    weights = [part.astype(jnp.bfloat16) for part in parts]
    weights = jnp.concatenate(weights, axis=1) if len(parts) > 1 else weights[0]
    out = jnp.dot(weights, values, preferred_element_type=jnp.float32)
    if before is not None:
        total = total + old_total * factor
        out = out + old_out * factor
    return out, new_max, total


def group_heads(k, q_ref, rows, keys, values, state, finish, first=False, **mask):
    scores, before = [None] * GROUP, [None] * GROUP
    for g in range(GROUP + AHEAD):
        if g < GROUP:
            h = k * GROUP + g
            scores[g] = score(q_ref[rows, head_columns(h)], keys)
            before[g] = None if first else load(h, rows, state)
        if g >= AHEAD:
            done = g - AHEAD
            finish(k * GROUP + done, attend(scores[done], values, before[done], **mask))


AHEAD = 8


def keep(h, rows, state, result):
    for ref, value in zip(state, result):
        ref[h, rows] = value


def head_columns(h):
    return pl.ds(pl.multiple_of(h * HD, HD), HD)


def suffix_own(q_ref, suf, state):
    rows = pl.ds(0, LOCAL)

    def body(k, _):
        keys, values = suf[0, :, head_columns(k)], suf[1, :, head_columns(k)]
        group_heads(k, q_ref, rows, keys, values, state, lambda h, r: keep(h, rows, state, r), first=True, causal=True)
        return 0
    lax.fori_loop(0, KVH, body, 0)


def suffix_other(q_ref, other, state, p):
    def run(rows, key_count):
        def body(k, _):
            keys, values = other[0, pl.ds(0, key_count), head_columns(k)], other[1, pl.ds(0, key_count), head_columns(k)]
            group_heads(k, q_ref, rows, keys, values, state, lambda h, r: keep(h, rows, state, r))
            return 0
        lax.fori_loop(0, KVH, body, 0)

    @pl.when(p == 0)
    def _():
        run(pl.ds(BLK, BLK), LOCAL)

    @pl.when(p == 1)
    def _():
        run(pl.ds(0, LOCAL), BLK)


def prefix_step(start, count, q_ref, paged, bias_ref, state):
    rows, span = pl.ds(0, LOCAL), pl.ds(start * CHUNK_KEYS, count * CHUNK_KEYS)

    def body(k, _):
        group_heads(k, q_ref, rows, paged[0, k, span], paged[1, k, span], state,
                    lambda h, r: keep(h, rows, state, r), bias=bias_ref[pl.ds(0, 1), span])
        return 0
    lax.fori_loop(0, KVH, body, 0)


def out_copy(k, q_ref, out_ref, out_sem):
    columns = pl.ds(pl.multiple_of(k * GROUP * HD, GROUP * HD), GROUP * HD)
    return pltpu.make_async_copy(q_ref.at[:, columns], out_ref.at[:, columns], out_sem.at[k])


def last_step(part, start, count, q_ref, paged, bias_ref, state, out_ref, out_sem):
    rows, span = pl.ds(0, LOCAL), pl.ds(start * CHUNK_KEYS, count * CHUNK_KEYS)

    def divide(h, result):
        out, _, total = result
        total = jnp.sum(total, axis=1, keepdims=True)
        q_ref[:, head_columns(h)] = (out / total).astype(jnp.bfloat16)

    def body(k, _):
        group_heads(k, q_ref, rows, paged[0, k, span], paged[1, k, span], state, divide, bias=bias_ref[pl.ds(0, 1), span])
        out_copy(k, q_ref, out_ref, out_sem).start()
        return 0
    lax.fori_loop(part * KVH // 2, (part + 1) * KVH // 2, body, 0)


def unfold(g, land, paged):
    for i in range(2):
        for lane in range(4):
            block = land[i, pl.ds(g * CHUNK_ROWS, CHUNK_ROWS), lane * HD:(lane + 1) * HD]
            block = block.astype(jnp.float32).reshape(PER_CHUNK, 2, PAGE, HD)
            for half in range(2):
                part = block[:, half].reshape(CHUNK_KEYS, HD).astype(jnp.bfloat16)
                paged[i, half * 4 + lane, pl.ds(g * CHUNK_KEYS, CHUNK_KEYS)] = part


def unfold_direct(part, land, paged):
    for g in DIRECT:
        for lane in range(4):
            block = land[part, pl.ds(g * CHUNK_ROWS, CHUNK_ROWS), lane * HD:(lane + 1) * HD]
            block = block.astype(jnp.float32).reshape(PER_CHUNK, 2, PAGE, HD)
            for i in range(2):
                paged[i, part * 4 + lane, pl.ds(g * CHUNK_KEYS, CHUNK_KEYS)] = block[:, i].reshape(CHUNK_KEYS, HD).astype(jnp.bfloat16)


def visible_bias(me, parent_ref, pages_ref, leaf_ref, length_ref, slot_ref, bias_ref):
    leaf = leaf_ref[me]
    mid = parent_ref[leaf]
    length = length_ref[me]
    width = slot_ref.shape[1]
    key = lax.broadcasted_iota(jnp.int32, (1, SLOTS * PAGE), 1)
    d = key >> 3
    g, item = d >> 4, d & 15
    iz, dc = item >> 1, item & 1
    dz = jnp.where((iz & 1) == 0, (iz >> 1) + 1, (8 - (iz >> 1)) & 7)
    dy, dx = chunk_step(g)
    holder = shifted(me + jnp.zeros_like(key), 2 - dy, 8 - dz, 4 - dx, 2 - dc).astype(jnp.float32)
    across = lax.broadcasted_iota(jnp.int32, (width, width), 1)
    down = lax.broadcasted_iota(jnp.int32, (width, width), 0)
    order = lax.broadcasted_iota(jnp.int32, (width, 1), 0)
    seen = jnp.zeros(key.shape, jnp.float32)
    first = 0
    for node in (0, 1 + mid, 1 + MIDS + leaf):
        count = pages_ref[node]
        row = (slot_ref[pl.ds(node, 1), :] >> 6).astype(jnp.float32)
        column = jnp.sum(jnp.where(across == down, jnp.broadcast_to(row, (width, width)), 0.0), axis=1, keepdims=True)
        tokens = jnp.clip(length - PAGE * (first + order), 0, PAGE)
        tokens = jnp.where(order < count, tokens, 0).astype(jnp.float32)
        match = column == holder
        seen = seen + jnp.sum(jnp.where(match, tokens, 0.0), axis=0, keepdims=True)
        first = first + count
    shown = (key & 7).astype(jnp.float32) < seen
    bias_ref[...] = jnp.broadcast_to(jnp.where(shown, 0.0, HIDDEN), bias_ref.shape)


def kernel(parent_ref, pages_ref, leaf_ref, length_ref, slot_hbm, pk_ref, pv_ref, q_hbm, sk_hbm, sv_hbm, out_ref,
           slot_ref, q_ref, suf, other, land, send, paged, acc_ref, max_ref, sum_ref, bias_ref, row_vec, row_smem,
           load_sem, row_sem, self_sem, send_sem, recv_sem, fwd_send, fwd_recv, suf_send, suf_recv, out_sem, near):
    me = lax.axis_index("store")
    p = lax.axis_index("pair")
    state = (acc_ref, max_ref, sum_ref)
    barrier = pltpu.get_barrier_semaphore()
    plane = [(dy, dx, dc) for dy in range(2) for dx in range(4) for dc in range(2) if (dy, dx, dc) != (0, 0, 0)]

    def tell(sem, dy, dz, dx, dc):
        pl.semaphore_signal(sem, inc=1, device_id=(shifted(me, dy, dz, dx, dc), (p + dy) & 1), device_id_type=MESH)

    load_slots = pltpu.make_async_copy(slot_hbm, slot_ref, row_sem)
    load_slots.start()
    for dy, dx, dc in plane:
        tell(barrier, dy, 0, dx, dc)
    for dz in range(1, 8):
        tell(barrier, 0, dz, 0, 0)
    pl.semaphore_signal(barrier, inc=1, device_id=(me, 1 - p), device_id_type=MESH)

    loads = [pltpu.make_async_copy(sk_hbm, suf.at[0], load_sem.at[0]),
             pltpu.make_async_copy(sv_hbm, suf.at[1], load_sem.at[1]),
             pltpu.make_async_copy(q_hbm, q_ref, load_sem.at[2])]
    for copy in loads:
        copy.start()

    load_slots.wait()
    places = slot_ref[...]
    mine = jnp.where(places >> 6 == me, places & 63, 0)
    best = jnp.max(mine, axis=1, keepdims=True)
    shape = (places.shape[0], 128)
    own_lane = lax.broadcasted_iota(jnp.int32, shape, 0) == lax.broadcasted_iota(jnp.int32, shape, 1)
    row_vec[...] = jnp.broadcast_to(jnp.sum(jnp.where(own_lane, best, 0), axis=0, keepdims=True), row_vec.shape)
    to_smem = pltpu.make_async_copy(row_vec, row_smem, row_sem)
    to_smem.start()
    to_smem.wait()

    near_part = [shifted(me & 57, 0, Z_ORDER[item // 2], 0, item % 2) for item in range(PER_CHUNK)]

    def chunk_target(g):
        dy, dx = chunk_step(g)
        return shifted(me & 70, dy, 0, dx, 0), (p + dy) & 1

    def pack(g, direct=False):
        far_part, _ = chunk_target(g)

        def put(i, item, upper, lower):
            start = pl.multiple_of(g * CHUNK_ROWS + item * ROWS, ROWS)
            send[i, pl.ds(start, ROWS), :] = jnp.concatenate([upper, lower], axis=0)

        def rows():
            for item in range(PER_CHUNK):
                leaf = leaf_ref[far_part + near_part[item]]
                mid = parent_ref[leaf]
                row = jnp.maximum(jnp.maximum(row_smem[0, 0], row_smem[0, 1 + mid]), row_smem[0, 1 + MIDS + leaf])
                yield item, jnp.clip(row, 0, PAGES_DEV - 1)

        if direct:
            for item, row in rows():
                keys, values = pk_ref[row], pv_ref[row]
                put(0, item, keys[:, :LANES], values[:, :LANES])
                put(1, item, keys[:, LANES:], values[:, LANES:])
            return

        for i, page_ref in ((0, pk_ref), (1, pv_ref)):
            @pl.when(p == i)
            def _():
                for item, row in rows():
                    page = page_ref[row]
                    put(i, item, page[:, :LANES], page[:, LANES:])

    def chunk_span(g):
        return pl.ds(pl.multiple_of(g * CHUNK_ROWS, CHUNK_ROWS), CHUNK_ROWS)

    def own_item(g):
        span = pl.ds(SELF_ITEM * ROWS, ROWS)
        return pltpu.make_async_copy(send.at[p, span], land.at[p, span], self_sem)

    def send_item(g, item, i, sem=None, extra=0):
        far_part, to_pair = chunk_target(g)
        span = pl.ds(pl.multiple_of(g * CHUNK_ROWS + item * ROWS, ROWS), ROWS)
        pltpu.make_async_remote_copy(
            send.at[i, span], land.at[i, span], send_sem.at[extra], recv_sem.at[g if sem is None else sem],
            device_id=(far_part + near_part[item], to_pair), device_id_type=MESH).start()

    def send_chunk(g, i, sem=None, extra=0):
        for item in range(PER_CHUNK):
            send_item(g, item, i, sem, extra)

    pack(0)
    pl.semaphore_wait(barrier, 8 + len(plane))
    for dy, dx, dc in plane:
        tell(near, dy, 0, dx, dc)
    for item in range(0, PER_CHUNK, 2):
        if item != SELF_ITEM:
            send_item(0, item, p)
    loads[0].wait()
    loads[1].wait()

    def suffix_copy(i, rows):
        return pltpu.make_async_remote_copy(suf.at[i, pl.ds(0, rows)], other.at[i, pl.ds(0, rows)], suf_send.at[i], suf_recv.at[i],
                                            device_id=(me, 1 - p), device_id_type=MESH)

    for rows, who in ((BLK, 0), (LOCAL, 1)):
        @pl.when(p == who)
        def _():
            suffix_copy(0, rows).start()
            suffix_copy(1, rows).start()
    own_item(0).start()
    pack(1)
    pl.semaphore_wait(near, len(plane))
    for item in range(1, PER_CHUNK, 2):
        send_item(0, item, p)
    send_chunk(1, p)

    def pack_send(g, _):
        pack(g)
        send_chunk(g, p)
        return 0

    def pack_send_lower(g, _):
        pack(g, direct=True)
        send_chunk(g, 0, DIRECT[0])
        return 0

    def send_upper(g, _):
        send_chunk(g, 1, DIRECT[1], 1)
        return 0

    lax.fori_loop(2, FIRST_DIRECT, pack_send, 0)
    lax.fori_loop(FIRST_DIRECT, CHUNKS, pack_send_lower, 0)
    lax.fori_loop(FIRST_DIRECT, CHUNKS, send_upper, 0)

    def forward(g):
        q = (p + g) & 1
        part = land.at[q, chunk_span(g)]
        return pltpu.make_async_remote_copy(part, part, fwd_send.at[g], fwd_recv.at[g], device_id=(me, 1 - p), device_id_type=MESH)

    def arrived(items, sem):
        part = send.at[0, pl.ds(0, items * ROWS)]
        pltpu.make_async_copy(part, part, sem).wait()

    def receive(g):
        arrived(PER_CHUNK - (g == 0), recv_sem.at[g])
        if g == 0:
            own_item(0).wait()
        forward(g).start()

    def whole(g):
        arrived(PER_CHUNK, fwd_recv.at[g])
        unfold(g, land, paged)

    def direct_part(part):
        arrived(len(DIRECT) * PER_CHUNK, recv_sem.at[DIRECT[part]])
        unfold_direct(part, land, paged)

    visible_bias(me, parent_ref, pages_ref, leaf_ref, length_ref, slot_ref, bias_ref)
    loads[2].wait()
    suffix_own(q_ref, suf, state)
    receive(0)
    receive(1)
    for rows, who in ((LOCAL, 0), (BLK, 1)):
        @pl.when(p == who)
        def _():
            for i in range(2):
                pltpu.make_async_copy(suf.at[i, pl.ds(0, rows)], suf.at[i, pl.ds(0, rows)], suf_recv.at[i]).wait()
    suffix_other(q_ref, other, state, p)
    receive(2)
    whole(0)
    receive(3)
    whole(1)
    prefix_step(0, 2, q_ref, paged, bias_ref, state)
    receive(4)
    whole(2)
    receive(5)
    whole(3)
    prefix_step(2, 2, q_ref, paged, bias_ref, state)
    whole(4)
    whole(5)
    prefix_step(4, 2, q_ref, paged, bias_ref, state)
    for part in range(2):
        direct_part(part)
        last_step(part, 6, 2, q_ref, paged, bias_ref, state, out_ref, out_sem)
    for k in range(KVH):
        out_copy(k, q_ref, out_ref, out_sem).wait()

    for g in range(CHUNKS):
        if g not in DIRECT:
            forward(g).wait_send()
    for rows, who in ((BLK, 0), (LOCAL, 1)):
        @pl.when(p == who)
        def _():
            suffix_copy(0, rows).wait_send()
            suffix_copy(1, rows).wait_send()
    arrived(SLOTS - 1, send_sem.at[0])
    arrived(len(DIRECT) * PER_CHUNK, send_sem.at[1])


def local(queries, suffix_keys, suffix_values, page_keys, page_values, leaf_parent, node_pages, page_slot, request_leaf, prefix_len):
    vmem = pl.BlockSpec(memory_space=pltpu.VMEM)
    smem = pl.BlockSpec(memory_space=pltpu.SMEM)
    anywhere = pl.BlockSpec(memory_space=pl.ANY)
    bf16, f32 = jnp.bfloat16, jnp.float32
    dma = pltpu.SemaphoreType.DMA
    out = pl.pallas_call(
        kernel,
        out_shape=jax.ShapeDtypeStruct((LOCAL, QH * HD), bf16),
        in_specs=[smem] * 4 + [anywhere] + [vmem] * 2 + [anywhere] * 3,
        out_specs=anywhere,
        scratch_shapes=[
            pltpu.VMEM(page_slot.shape, jnp.int32),
            pltpu.VMEM((LOCAL, QH * HD), bf16),
            pltpu.VMEM((2, LOCAL, KVH * HD), bf16),
            pltpu.VMEM((2, LOCAL, KVH * HD), bf16),
            pltpu.VMEM((2, SLOTS * ROWS, LANES), bf16),
            pltpu.VMEM((2, SLOTS * ROWS, LANES), bf16),
            pltpu.VMEM((2, KVH, SLOTS * PAGE, HD), bf16),
            pltpu.VMEM((QH, LOCAL, HD), f32),
            pltpu.VMEM((QH, LOCAL, HD), f32),
            pltpu.VMEM((QH, LOCAL, HD), f32),
            pltpu.VMEM((8, SLOTS * PAGE), f32),
            pltpu.VMEM((8, 128), jnp.int32),
            pltpu.SMEM((8, 128), jnp.int32),
            dma((3,)), dma, dma, dma((2,)), dma((CHUNKS,)), dma((CHUNKS,)), dma((CHUNKS,)), dma((2,)), dma((2,)), dma((KVH,)),
            pltpu.SemaphoreType.REGULAR,
        ],
        compiler_params=pltpu.CompilerParams(collective_id=1, has_side_effects=True, vmem_limit_bytes=60 * 2**20),
    )(leaf_parent, node_pages, request_leaf, prefix_len, page_slot, page_keys, page_values,
      queries.reshape(LOCAL, QH * HD), suffix_keys.reshape(LOCAL, KVH * HD), suffix_values.reshape(LOCAL, KVH * HD))
    return out.reshape(queries.shape)


def solution(mesh):
    big = P("store", "pair", None, None, None)
    return jax.shard_map(
        local, mesh=mesh,
        in_specs=(big, big, big, P("store", None, None), P("store", None, None), P(), P(), P(), P(), P()),
        out_specs=big, check_vma=False)
```
